32 devices in a mesh: fsdp: 8 (over y, x, core), tensor: 4 (over z).
Axes of the slice: x: 2, y: 2, z: 4, core: 2. Of those that a mesh axis runs over, the one named last changes fastest.
Arguments:
- tokens: bfloat16 [1024, 16384], P('fsdp', 'tensor'), may hold values from -6 to 6
- seg_ids: int32 [8, 128], P('fsdp'), may hold values from 0 to 7, never falling along the last dimension, each value on 1 to 64 neighbouring positions
- key_weight: bfloat16 [512, 16384], P('fsdp', 'tensor'), may hold values from -0.046875 to 0.046875
- key_grad: bfloat16 [1024, 512], P('fsdp'), may hold values from -6 to 6
Outputs:
- keys: bfloat16 [1024, 512], P('fsdp')
- grad_tokens: bfloat16 [1024, 16384], P('fsdp', 'tensor')
- grad_key_weight: float32 [512, 16384], P('fsdp', 'tensor')
The draws below stay inside these ranges and needn't reach their ends.
Inputs may be any that keep to these rules, and one draw needn't show every extreme that they name: `seg_ids`: within each window the ids never fall; each document spans 1 to 64 tokens, one exactly 64.
All inputs are finite; a program needn't handle non-finite values.
Results may differ from the reference program's by a relative error of at most 0.0041.
Values may be sent and summed in bfloat16 or wider, within the bound.
A program may use at most 64 MiB of HBM per device.

```python
import math
import jax
import jax.numpy as jnp
import numpy as np
from jax import lax

D = 16384
KV_HEADS = 4
HEAD = 128
TOK_DEV = 128
TOKENS = 1024
N_FSDP = 8


def strengthened(values, key, source, target, shards_of, factor):
    owner, partner = [(jnp.arange(values.shape[position]) // (values.shape[position] // shards_of)).reshape([-1 if axis == position else 1 for axis in range(values.ndim)]) for position in (source, target)]
    chosen = jax.random.permutation(key, shards_of)[partner]
    strong = (owner == chosen) | (owner == (partner + shards_of // 2) % shards_of)
    return jnp.where(strong, factor * values, values)


def level_of(stream_key, dims, pieces, least, high):
    loudness, own = 1.0, jax.random.fold_in(stream_key, 6)
    for axis_at, shards_of in pieces:
        draws = jnp.exp(jax.random.uniform(jax.random.fold_in(own, axis_at), (shards_of,), jnp.float32, least / len(pieces), high / len(pieces)))
        loudness = loudness * jnp.repeat(draws, dims[axis_at] // shards_of).reshape([-1 if axis == axis_at else 1 for axis in range(len(dims))])
    return loudness


def split_up(amount, total, limit, lean):
    loads = [(1 << 20) // math.isqrt(rank ** lean) + 1 for rank in range(2, amount + 1)]
    spare, counts = total - limit - (amount - 1), [1] * (amount - 1)
    while spare > 0:
        candidates = [i for i in range(amount - 1) if counts[i] < limit]
        pool, remaining = sum([loads[i] for i in candidates]), spare
        for i in candidates:
            extra = min(limit - counts[i], max(1, remaining * loads[i] // pool), spare)
            counts[i] = counts[i] + extra
            spare = spare - extra
    return np.array([limit] + counts)


def uneven(key, count, total, limit, skew):
    if count == 2:
        one = jax.random.randint(key, (), max(1, total - limit), min(limit, total - 1) + 1)
        return jnp.stack([one, total - one])
    sizes = jnp.asarray(split_up(count, total, limit, skew), jnp.int32)
    pairs = (count - 1) // 2
    donor, sink = sizes[1:1 + 2 * pairs:2], sizes[2:2 + 2 * pairs:2]
    margin = jnp.minimum(donor - 1, limit - sink)
    shifted = jax.random.randint(jax.random.fold_in(key, 1), (pairs,), 0, 1 << 20) % (margin + 1)
    sizes = sizes.at[1:1 + 2 * pairs:2].set(donor - shifted).at[2:2 + 2 * pairs:2].set(sink + shifted)
    return sizes[jax.random.permutation(jax.random.fold_in(key, 2), count)]


def centred(stream_key, dims, scale, reach, pieces=(), kind=jnp.bfloat16):
    result = jax.random.normal(stream_key, dims, jnp.float32) * scale
    if len(pieces) > 0:
        result = level_of(stream_key, dims, pieces, -0.22, 0.18) * result
    return jnp.clip(result, min=-reach, max=reach).astype(kind)


def bell_draw_with(stream_key, extent, spread, most, shards, heavy, kind=jnp.bfloat16):
    drawn = spread * jax.random.normal(stream_key, extent, jnp.float32)
    if shards:
        drawn = drawn * level_of(stream_key, extent, shards, -0.22, 0.18)
    return jnp.clip(strengthened(drawn, jax.random.fold_in(stream_key, 3), *heavy), -most, most).astype(kind)


def setup_inputs(seed: int = 0) -> dict:
    splits = jax.random.split(jax.random.key(seed), 5)
    tokens = centred(splits[0], (TOKENS, D), 1.0, 6.0, ((0, 8), (1, 4)))
    seg_ids = jax.vmap(lambda own: jnp.searchsorted(jnp.cumsum(uneven(own, 8, TOK_DEV, TOK_DEV // 2, 2)), jnp.arange(TOK_DEV), side="right"))(jax.random.split(splits[1], N_FSDP)).reshape((N_FSDP, TOK_DEV)).astype(jnp.int32)
    key_weight = centred(splits[2], (KV_HEADS * HEAD, D), D ** -0.5, 0.046875, ((0, 8), (1, 4)))
    key_grad = bell_draw_with(splits[3], (TOKENS, KV_HEADS * HEAD), 1.0, 6.0, ((0, 8),), (0, 1, 8, 2.0))
    return {"tokens": tokens, "seg_ids": seg_ids, "key_weight": key_weight, "key_grad": key_grad}


def doc_positions(seg_ids):
    width = seg_ids.shape[1]
    index = jnp.arange(width, dtype=jnp.int32)
    change = jnp.concatenate([jnp.ones((seg_ids.shape[0], 1), bool), seg_ids[:, 1:] != seg_ids[:, :-1]], axis=1)
    first = lax.cummax(jnp.where(change, index[None, :], 0).astype(jnp.int32), axis=1)
    return (index[None, :] - first).reshape(-1)


def angles(positions, half):
    freq = 500000.0 ** (-2.0 * jnp.arange(half, dtype=jnp.float32) / (2 * half))
    turn = positions.astype(jnp.float32)[:, None] * freq[None, :]
    return jnp.cos(turn)[:, None, :], jnp.sin(turn)[:, None, :]


def rotate(field, cosine, sine, sign):
    rows = field.shape[0]
    shaped = field.reshape(rows, -1, HEAD)
    first, second = shaped[..., :HEAD // 2], shaped[..., HEAD // 2:]
    out = jnp.concatenate([first * cosine - sign * second * sine, second * cosine + sign * first * sine], axis=-1)
    return out.reshape(rows, -1)


def reference(tokens, seg_ids, key_weight, key_grad):
    cosine, sine = angles(doc_positions(seg_ids), HEAD // 2)
    kraw = lax.dot_general(tokens, key_weight, (((1,), (1,)), ((), ())), preferred_element_type=jnp.float32)
    keys = rotate(kraw, cosine, sine, 1.0).astype(jnp.bfloat16)
    kback = rotate(key_grad.astype(jnp.float32), cosine, sine, -1.0).astype(jnp.bfloat16)
    grad_tokens = jnp.dot(kback, key_weight, preferred_element_type=jnp.float32).astype(jnp.bfloat16)
    grad_key_weight = lax.dot_general(kback, tokens, (((0,), (0,)), ((), ())), preferred_element_type=jnp.float32)
    return keys, grad_tokens, grad_key_weight
```

```python
import functools

import jax
import jax.numpy as jnp
import numpy as np
from jax import lax
from jax.experimental import pallas as pl
from jax.experimental.pallas import tpu as pltpu
from jax.sharding import PartitionSpec as P

HEAD = 128
MESH = pl.DeviceIdType.MESH
F32 = jnp.float32
BF16 = jnp.bfloat16


def doc_positions(segments):
    width = segments.shape[0]
    index = jnp.arange(width, dtype=jnp.int32)
    change = jnp.concatenate([jnp.ones((1,), bool), segments[1:] != segments[:-1]])
    first = lax.cummax(jnp.where(change, index, 0))
    return index - first


def angles(positions, half):
    freq = 500000.0 ** (-2.0 * jnp.arange(half, dtype=jnp.float32) / (2 * half))
    turn = positions.astype(jnp.float32)[:, None] * freq[None, :]
    return (jnp.cos(turn)[:, None, :], jnp.sin(turn)[:, None, :])


def rotate(field, cosine, sine, sign):
    rows = field.shape[0]
    shaped = field.reshape(rows, -1, HEAD)
    first, second = (shaped[..., : HEAD // 2], shaped[..., HEAD // 2 :])
    out = jnp.concatenate(
        [first * cosine - sign * second * sine, second * cosine + sign * first * sine], axis=-1
    )
    return out.reshape(rows, -1)


def plain_body(tokens, seg_ids, key_weight, key_grad):
    cosine, sine = angles(doc_positions(seg_ids[0]), HEAD // 2)
    weights = lax.all_gather(key_weight, "fsdp", axis=0, tiled=True)
    partial_value = lax.dot_general(
        tokens, weights, (((1,), (1,)), ((), ())), preferred_element_type=jnp.float32
    )
    kraw = lax.psum(partial_value, "tensor")
    keys = rotate(kraw, cosine, sine, 1.0).astype(jnp.bfloat16)
    kback = rotate(key_grad.astype(jnp.float32), cosine, sine, -1.0).astype(jnp.bfloat16)
    grad_tokens = jnp.dot(kback, weights, preferred_element_type=jnp.float32)
    grad_key_weight = lax.psum_scatter(
        lax.dot_general(
            kback, tokens, (((0,), (0,)), ((), ())), preferred_element_type=jnp.float32
        ),
        "fsdp",
        scatter_dimension=0,
        tiled=True,
    )
    return (keys, grad_tokens.astype(jnp.bfloat16), grad_key_weight)


def turned(block, cosine, signed_sine):
    return block * cosine + pltpu.roll(block, HEAD // 2, 1) * signed_sine


def cube_kernel(
    nz, tile,
    tok, seg, w, kg, freq,
    keys_out, gtok_out, gw_out,
    wall, tok_sib, kbt, kbt_sib, kb, cos_s, sin_s, snd, comb, from_x, from_y, fin_x, fin_y,
    kraw, zin, keyb,
    s_ag, r_ag, s_sib, r_sib, s_rs, r_rs, s_z, r_z, s_k, r_k,
):
    f, t = lax.axis_index("fsdp"), lax.axis_index("tensor")
    y, x, c = f // 4, (f // 2) % 2, f % 2
    xn = y * 4 + (1 - x) * 2 + c
    yn = (1 - y) * 4 + x * 2 + c
    dg = (1 - y) * 4 + (1 - x) * 2 + c
    sib = y * 4 + x * 2 + (1 - c)
    rows, depth = w.shape
    half = rows // 2
    toks, heads = tok.shape[0], kg.shape[1] // HEAD
    peers = [lax.rem(t + d, nz) for d in range(1, nz)]

    barrier = pltpu.get_barrier_semaphore()
    for g in (xn, yn, sib):
        pl.semaphore_signal(barrier, inc=1, device_id=(g, t), device_id_type=MESH)
    for p in peers:
        pl.semaphore_signal(barrier, inc=1, device_id=(f, p), device_id_type=MESH)
    pl.semaphore_wait(barrier, 3 + len(peers))

    pending = []

    def send(src, dst, ssem, rsem, g, p):
        copy = pltpu.make_async_remote_copy(
            src_ref=src, dst_ref=dst, send_sem=ssem, recv_sem=rsem,
            device_id=(g, p), device_id_type=MESH,
        )
        copy.start()
        pending.append(copy)
        return copy

    def shard_half(g, h):
        return wall.at[pl.ds(pl.multiple_of(g * rows + h * half, half), half)]

    def w_half(h):
        return w.at[pl.ds(h * half, half)]

    ax, ay = [None, None], [None, None]
    ax[0] = send(w_half(0), shard_half(f, 0), s_ag.at[0], r_ag.at[0], xn, t)
    ay[1] = send(w_half(1), shard_half(f, 1), s_ag.at[3], r_ag.at[3], yn, t)
    tok_copy = send(tok, tok_sib, s_sib.at[0], r_sib.at[0], sib, t)
    ax[1] = send(w_half(1), shard_half(f, 1), s_ag.at[1], r_ag.at[1], xn, t)
    ay[0] = send(w_half(0), shard_half(f, 0), s_ag.at[2], r_ag.at[2], yn, t)
    own_rows = pl.ds(pl.multiple_of(f * rows, rows), rows)
    own_copy = send(w, wall.at[own_rows], s_sib.at[2], r_sib.at[2], sib, t)

    ids = jnp.broadcast_to(seg[...].astype(F32), (toks, toks))
    row = lax.broadcasted_iota(jnp.int32, (toks, toks), 0)
    col = lax.broadcasted_iota(jnp.int32, (toks, toks), 1)
    same = jnp.where((ids == ids.T) & (col < row), 1.0, 0.0)
    position = jnp.sum(same, axis=1, keepdims=True)
    turn = position * freq[...]
    lane = lax.broadcasted_iota(jnp.int32, (toks, HEAD), 1)
    cosine = jnp.cos(turn)
    sine = jnp.sin(turn)
    sine = jnp.where(lane < HEAD // 2, -sine, sine)
    cos_s[...] = cosine
    sin_s[...] = sine
    for h in range(heads):
        lanes = pl.ds(h * HEAD, HEAD)
        back = turned(kg[:, lanes].astype(F32), cosine, -sine).astype(BF16)
        kb[:, lanes] = back
        kbt[lanes, :] = back.astype(F32).T.astype(BF16)
    kb_copy = send(kbt, kbt_sib, s_sib.at[1], r_sib.at[1], sib, t)
    wall[own_rows, :] = w[...]

    tok_copy.wait_recv()
    kb_copy.wait_recv()
    picked = []
    for g in (dg, xn, yn, f):
        at = pl.ds(pl.multiple_of(g * rows, rows), rows)
        picked.append(jnp.concatenate([kbt[at, :], kbt_sib[at, :]], axis=1))
    left = jnp.concatenate(picked, axis=0)

    @pl.loop(0, depth // tile)
    def _(i):
        lanes = pl.ds(pl.multiple_of(i * tile, tile), tile)
        right = jnp.concatenate([tok[:, lanes], tok_sib[:, lanes]], axis=0)
        part = jnp.dot(left, right, preferred_element_type=F32)
        snd[0, :, lanes] = part[:rows].astype(BF16)
        snd[1, :half, lanes] = part[rows : rows + half].astype(BF16)
        comb[0, :, lanes] = part[rows + half : 2 * rows]
        comb[1, :, lanes] = part[2 * rows : 2 * rows + half]
        snd[2, half:, lanes] = part[2 * rows + half : 3 * rows].astype(BF16)
        gw_out[:, lanes] = part[3 * rows :]

    sib_waits = [own_copy]

    def to_sib(g, h, n):
        sib_waits.append(
            send(shard_half(g, h), shard_half(g, h), s_sib.at[n], r_sib.at[n], sib, t)
        )

    ax[0].wait_recv()
    ad0 = send(shard_half(xn, 0), shard_half(xn, 0), s_ag.at[4], r_ag.at[4], yn, t)
    ay[1].wait_recv()
    ad1 = send(shard_half(yn, 1), shard_half(yn, 1), s_ag.at[5], r_ag.at[5], xn, t)
    to_sib(xn, 0, 3)
    to_sib(yn, 1, 4)

    top, bottom = pl.ds(0, half), pl.ds(half, half)
    rdx = send(snd.at[0, top], from_x, s_rs.at[0], r_rs.at[0], xn, t)
    rdy = send(snd.at[0, bottom], from_y, s_rs.at[1], r_rs.at[1], yn, t)
    fx0 = send(snd.at[1, top], fin_x.at[top], s_rs.at[2], r_rs.at[2], xn, t)
    fy1 = send(snd.at[2, bottom], fin_y.at[bottom], s_rs.at[3], r_rs.at[3], yn, t)

    ax[1].wait_recv()
    to_sib(xn, 1, 5)
    ay[0].wait_recv()
    to_sib(yn, 0, 6)
    ad0.wait_recv()
    to_sib(dg, 0, 7)
    ad1.wait_recv()
    to_sib(dg, 1, 8)
    for copy in sib_waits:
        copy.wait_recv()

    kraw[...] = jnp.zeros_like(kraw)

    @pl.loop(0, depth // tile)
    def _(i):
        lanes = pl.ds(pl.multiple_of(i * tile, tile), tile)
        kraw[...] += lax.dot_general(
            tok[:, lanes], wall[:, lanes], (((1,), (1,)), ((), ())), preferred_element_type=F32
        )

    share = toks // nz

    def rows_of(p):
        return pl.ds(pl.multiple_of(p * share, share), share)

    z_copies = [
        send(kraw.at[rows_of(p)], zin.at[d], s_z.at[d], r_z.at[d], f, p)
        for d, p in enumerate(peers)
    ]

    rdx.wait_recv()
    snd[2, :half] = (comb[1] + from_x[...].astype(F32)).astype(BF16)
    fy0 = send(snd.at[2, top], fin_y.at[top], s_rs.at[4], r_rs.at[4], yn, t)
    rdy.wait_recv()
    snd[1, half:] = (comb[0] + from_y[...].astype(F32)).astype(BF16)
    fx1 = send(snd.at[1, bottom], fin_x.at[bottom], s_rs.at[5], r_rs.at[5], xn, t)

    mine = rows_of(t)
    total = kraw[mine, :]
    for d, copy in enumerate(z_copies):
        copy.wait_recv()
        total = total + zin[d]
    cosine, sine = cos_s[mine, :], sin_s[mine, :]
    for h in range(heads):
        keyb[mine, h * HEAD : (h + 1) * HEAD] = turned(
            total[:, h * HEAD : (h + 1) * HEAD], cosine, sine
        ).astype(BF16)
    k_copies = [
        send(keyb.at[mine], keyb.at[mine], s_k.at[d], r_k.at[d], f, p)
        for d, p in enumerate(peers)
    ]

    @pl.loop(0, depth // tile)
    def _(i):
        lanes = pl.ds(pl.multiple_of(i * tile, tile), tile)
        gtok_out[:, lanes] = jnp.dot(
            kb[...], wall[:, lanes], preferred_element_type=F32
        ).astype(BF16)

    for copy in k_copies:
        copy.wait_recv()
    keys_out[...] = keyb[...]

    fx0.wait_recv()
    gw_out[:half] += fin_x[:half].astype(F32)
    fy1.wait_recv()
    gw_out[half:] += fin_y[half:].astype(F32)
    fy0.wait_recv()
    gw_out[:half] += fin_y[:half].astype(F32)
    fx1.wait_recv()
    gw_out[half:] += fin_x[half:].astype(F32)
    for copy in pending:
        copy.wait_send()


def cube_body(nz, tokens, seg_ids, key_weight, key_grad):
    toks, depth = tokens.shape
    rows, width = key_weight.shape[0], key_grad.shape[1]
    half = rows // 2
    tile = min(512, depth)
    freq = np.float32(500000.0) ** (-2.0 * np.arange(HEAD // 2, dtype=np.float32) / HEAD)
    freq = jnp.asarray(np.tile(freq.astype(np.float32), 2)[None, :])
    vmem = pl.BlockSpec(memory_space=pltpu.VMEM)
    dma = pltpu.SemaphoreType.DMA
    far = max(nz - 1, 1)
    return pl.pallas_call(
        functools.partial(cube_kernel, nz, tile),
        out_shape=(
            jax.ShapeDtypeStruct((toks, width), BF16),
            jax.ShapeDtypeStruct((toks, depth), BF16),
            jax.ShapeDtypeStruct((rows, depth), F32),
        ),
        in_specs=[vmem] * 5,
        out_specs=(vmem,) * 3,
        scratch_shapes=[
            pltpu.VMEM((width, depth), BF16),
            pltpu.VMEM((toks, depth), BF16),
            pltpu.VMEM((width, toks), BF16),
            pltpu.VMEM((width, toks), BF16),
            pltpu.VMEM((toks, width), BF16),
            pltpu.VMEM((toks, HEAD), F32),
            pltpu.VMEM((toks, HEAD), F32),
            pltpu.VMEM((3, rows, depth), BF16),
            pltpu.VMEM((2, half, depth), F32),
            pltpu.VMEM((half, depth), BF16),
            pltpu.VMEM((half, depth), BF16),
            pltpu.VMEM((rows, depth), BF16),
            pltpu.VMEM((rows, depth), BF16),
            pltpu.VMEM((toks, width), F32),
            pltpu.VMEM((far, toks // nz, width), F32),
            pltpu.VMEM((toks, width), BF16),
            dma((6,)), dma((6,)),
            dma((9,)), dma((9,)),
            dma((6,)), dma((6,)),
            dma((far,)), dma((far,)),
            dma((far,)), dma((far,)),
        ],
        compiler_params=pltpu.CompilerParams(
            collective_id=0, has_side_effects=True, vmem_limit_bytes=40 * 1024 * 1024
        ),
        cost_estimate=pl.CostEstimate(
            flops=6 * toks * width * depth,
            bytes_accessed=4 * toks * depth + 6 * rows * depth,
            transcendentals=2 * toks * HEAD,
        ),
    )(tokens, seg_ids, key_weight, key_grad, freq)


def solution(mesh):
    nz = mesh.shape["tensor"]
    body = plain_body
    if mesh.shape["fsdp"] == 8 and nz <= 8:
        body = functools.partial(cube_body, nz)
    placed = (P("fsdp", "tensor"), P("fsdp", None), P("fsdp", "tensor"), P("fsdp", None))
    return jax.shard_map(
        body,
        mesh=mesh,
        in_specs=placed,
        out_specs=(P("fsdp", None), P("fsdp", "tensor"), P("fsdp", "tensor")),
        check_vma=False,
    )
```

```python
import functools

import jax
import jax.numpy as jnp
import numpy as np
from jax import lax
from jax.experimental import pallas as pl
from jax.experimental.pallas import tpu as pltpu
from jax.sharding import PartitionSpec as P

HEAD = 128
MESH = pl.DeviceIdType.MESH
F32 = jnp.float32
BF16 = jnp.bfloat16


def doc_positions(segments):
    width = segments.shape[0]
    index = jnp.arange(width, dtype=jnp.int32)
    change = jnp.concatenate([jnp.ones((1,), bool), segments[1:] != segments[:-1]])
    first = lax.cummax(jnp.where(change, index, 0))
    return index - first


def angles(positions, half):
    freq = 500000.0 ** (-2.0 * jnp.arange(half, dtype=jnp.float32) / (2 * half))
    turn = positions.astype(jnp.float32)[:, None] * freq[None, :]
    return (jnp.cos(turn)[:, None, :], jnp.sin(turn)[:, None, :])


def rotate(field, cosine, sine, sign):
    rows = field.shape[0]
    shaped = field.reshape(rows, -1, HEAD)
    first, second = (shaped[..., : HEAD // 2], shaped[..., HEAD // 2 :])
    out = jnp.concatenate(
        [first * cosine - sign * second * sine, second * cosine + sign * first * sine], axis=-1
    )
    return out.reshape(rows, -1)


def plain_body(tokens, seg_ids, key_weight, key_grad):
    cosine, sine = angles(doc_positions(seg_ids[0]), HEAD // 2)
    weights = lax.all_gather(key_weight, "fsdp", axis=0, tiled=True)
    partial_value = lax.dot_general(
        tokens, weights, (((1,), (1,)), ((), ())), preferred_element_type=jnp.float32
    )
    kraw = lax.psum(partial_value, "tensor")
    keys = rotate(kraw, cosine, sine, 1.0).astype(jnp.bfloat16)
    kback = rotate(key_grad.astype(jnp.float32), cosine, sine, -1.0).astype(jnp.bfloat16)
    grad_tokens = jnp.dot(kback, weights, preferred_element_type=jnp.float32)
    grad_key_weight = lax.psum_scatter(
        lax.dot_general(
            kback, tokens, (((0,), (0,)), ((), ())), preferred_element_type=jnp.float32
        ),
        "fsdp",
        scatter_dimension=0,
        tiled=True,
    )
    return (keys, grad_tokens.astype(jnp.bfloat16), grad_key_weight)


def turned(block, cosine, signed_sine):
    return block * cosine + pltpu.roll(block, HEAD // 2, 1) * signed_sine


def cube_kernel(
    nz, tile,
    tok_hbm, seg_hbm, w, kg_hbm, freq_hbm,
    keys_hbm, gtok_hbm, gw_hbm,
    keyb, gtok_out, gw_out, tok, seg, kg, freq, wall, tok_sib, kbt, kbt_sib, kb, cos_s, sin_s, snd, comb, from_x, from_y, fin_x, fin_y,
    kraw, zin,
    s_ag, r_ag, s_sib, r_sib, s_rs, r_rs, s_z, r_z, s_k, r_k, s_in, s_out,
):
    f, t = lax.axis_index("fsdp"), lax.axis_index("tensor")
    y, x, c = f // 4, (f // 2) % 2, f % 2
    xn = y * 4 + (1 - x) * 2 + c
    yn = (1 - y) * 4 + x * 2 + c
    dg = (1 - y) * 4 + (1 - x) * 2 + c
    sib = y * 4 + x * 2 + (1 - c)
    rows, depth = w.shape
    half = rows // 2
    toks, heads = tok.shape[0], kg.shape[1] // HEAD
    peers = [lax.rem(t + d, nz) for d in range(1, nz)]

    barrier = pltpu.get_barrier_semaphore()
    for g in (xn, yn, sib):
        pl.semaphore_signal(barrier, inc=1, device_id=(g, t), device_id_type=MESH)
    for p in peers:
        pl.semaphore_signal(barrier, inc=1, device_id=(f, p), device_id_type=MESH)
    own_rows = pl.ds(pl.multiple_of(f * rows, rows), rows)
    loads = [
        pltpu.make_async_copy(src, dst, s_in.at[n])
        for n, (src, dst) in enumerate(
            ((seg_hbm, seg), (freq_hbm, freq), (kg_hbm, kg), (tok_hbm, tok), (w, wall.at[own_rows]))
        )
    ]
    for load in loads:
        load.start()
    pl.semaphore_wait(barrier, 3 + len(peers))

    pending = []

    def send(src, dst, ssem, rsem, g, p):
        copy = pltpu.make_async_remote_copy(
            src_ref=src, dst_ref=dst, send_sem=ssem, recv_sem=rsem,
            device_id=(g, p), device_id_type=MESH,
        )
        copy.start()
        pending.append(copy)
        return copy

    def shard_half(g, h):
        return wall.at[pl.ds(pl.multiple_of(g * rows + h * half, half), half)]

    def w_half(h):
        return w.at[pl.ds(h * half, half)]

    ax, ay = [None, None], [None, None]
    ax[0] = send(w_half(0), shard_half(f, 0), s_ag.at[0], r_ag.at[0], xn, t)
    ay[1] = send(w_half(1), shard_half(f, 1), s_ag.at[3], r_ag.at[3], yn, t)
    tok_copy = send(tok_hbm, tok_sib, s_sib.at[0], r_sib.at[0], sib, t)
    ax[1] = send(w_half(1), shard_half(f, 1), s_ag.at[1], r_ag.at[1], xn, t)
    ay[0] = send(w_half(0), shard_half(f, 0), s_ag.at[2], r_ag.at[2], yn, t)
    own_copy = send(w, wall.at[own_rows], s_sib.at[2], r_sib.at[2], sib, t)

    for load in loads[:3]:
        load.wait()
    ids = jnp.broadcast_to(seg[...].astype(F32), (toks, toks))
    row = lax.broadcasted_iota(jnp.int32, (toks, toks), 0)
    col = lax.broadcasted_iota(jnp.int32, (toks, toks), 1)
    same = jnp.where((ids == ids.T) & (col < row), 1.0, 0.0)
    position = jnp.sum(same, axis=1, keepdims=True)
    turn = position * freq[...]
    lane = lax.broadcasted_iota(jnp.int32, (toks, HEAD), 1)
    cosine = jnp.cos(turn)
    sine = jnp.sin(turn)
    sine = jnp.where(lane < HEAD // 2, -sine, sine)
    cos_s[...] = cosine
    sin_s[...] = sine
    for h in range(heads):
        lanes = pl.ds(h * HEAD, HEAD)
        back = turned(kg[:, lanes].astype(F32), cosine, -sine).astype(BF16)
        kb[:, lanes] = back
        kbt[lanes, :] = back.astype(F32).T.astype(BF16)
    kb_copy = send(kbt, kbt_sib, s_sib.at[1], r_sib.at[1], sib, t)

    for load in loads[3:]:
        load.wait()
    tok_copy.wait_recv()
    kb_copy.wait_recv()
    picked = []
    for g in (dg, xn, yn, f):
        at = pl.ds(pl.multiple_of(g * rows, rows), rows)
        picked.append(jnp.concatenate([kbt[at, :], kbt_sib[at, :]], axis=1))
    left = jnp.concatenate(picked, axis=0)

    @pl.loop(0, depth // tile)
    def _(i):
        lanes = pl.ds(pl.multiple_of(i * tile, tile), tile)
        right = jnp.concatenate([tok[:, lanes], tok_sib[:, lanes]], axis=0)
        part = jnp.dot(left, right, preferred_element_type=F32)
        snd[0, :, lanes] = part[:rows].astype(BF16)
        snd[1, :half, lanes] = part[rows : rows + half].astype(BF16)
        comb[0, :, lanes] = part[rows + half : 2 * rows]
        comb[1, :, lanes] = part[2 * rows : 2 * rows + half]
        snd[2, half:, lanes] = part[2 * rows + half : 3 * rows].astype(BF16)
        gw_out[:, lanes] = part[3 * rows :]

    sib_waits = [own_copy]

    def to_sib(g, h, n):
        sib_waits.append(
            send(shard_half(g, h), shard_half(g, h), s_sib.at[n], r_sib.at[n], sib, t)
        )

    ax[0].wait_recv()
    ad0 = send(shard_half(xn, 0), shard_half(xn, 0), s_ag.at[4], r_ag.at[4], yn, t)
    ay[1].wait_recv()
    ad1 = send(shard_half(yn, 1), shard_half(yn, 1), s_ag.at[5], r_ag.at[5], xn, t)
    to_sib(xn, 0, 3)
    to_sib(yn, 1, 4)

    top, bottom = pl.ds(0, half), pl.ds(half, half)
    rdx = send(snd.at[0, top], from_x, s_rs.at[0], r_rs.at[0], xn, t)
    rdy = send(snd.at[0, bottom], from_y, s_rs.at[1], r_rs.at[1], yn, t)
    fx0 = send(snd.at[1, top], fin_x.at[top], s_rs.at[2], r_rs.at[2], xn, t)
    fy1 = send(snd.at[2, bottom], fin_y.at[bottom], s_rs.at[3], r_rs.at[3], yn, t)

    ax[1].wait_recv()
    to_sib(xn, 1, 5)
    ay[0].wait_recv()
    to_sib(yn, 0, 6)
    ad0.wait_recv()
    to_sib(dg, 0, 7)
    ad1.wait_recv()
    to_sib(dg, 1, 8)
    for copy in sib_waits:
        copy.wait_recv()

    kraw[...] = jnp.zeros_like(kraw)

    @pl.loop(0, depth // tile)
    def _(i):
        lanes = pl.ds(pl.multiple_of(i * tile, tile), tile)
        kraw[...] += lax.dot_general(
            tok[:, lanes], wall[:, lanes], (((1,), (1,)), ((), ())), preferred_element_type=F32
        )

    share = toks // nz

    def rows_of(p):
        return pl.ds(pl.multiple_of(p * share, share), share)

    z_copies = [
        send(kraw.at[rows_of(p)], zin.at[d], s_z.at[d], r_z.at[d], f, p)
        for d, p in enumerate(peers)
    ]

    rdx.wait_recv()
    snd[2, :half] = (comb[1] + from_x[...].astype(F32)).astype(BF16)
    fy0 = send(snd.at[2, top], fin_y.at[top], s_rs.at[4], r_rs.at[4], yn, t)
    rdy.wait_recv()
    snd[1, half:] = (comb[0] + from_y[...].astype(F32)).astype(BF16)
    fx1 = send(snd.at[1, bottom], fin_x.at[bottom], s_rs.at[5], r_rs.at[5], xn, t)

    mine = rows_of(t)
    total = kraw[mine, :]
    for d, copy in enumerate(z_copies):
        copy.wait_recv()
        total = total + zin[d]
    cosine, sine = cos_s[mine, :], sin_s[mine, :]
    for h in range(heads):
        keyb[mine, h * HEAD : (h + 1) * HEAD] = turned(
            total[:, h * HEAD : (h + 1) * HEAD], cosine, sine
        ).astype(BF16)
    k_copies = [
        send(keyb.at[mine], keyb.at[mine], s_k.at[d], r_k.at[d], f, p)
        for d, p in enumerate(peers)
    ]

    @pl.loop(0, depth // tile)
    def _(i):
        lanes = pl.ds(pl.multiple_of(i * tile, tile), tile)
        gtok_out[:, lanes] = jnp.dot(
            kb[...], wall[:, lanes], preferred_element_type=F32
        ).astype(BF16)

    moves = [pltpu.make_async_copy(gtok_out, gtok_hbm, s_out.at[0])]
    moves[0].start()
    for copy in k_copies:
        copy.wait_recv()
    moves.append(pltpu.make_async_copy(keyb, keys_hbm, s_out.at[1]))
    moves[1].start()

    fx0.wait_recv()
    gw_out[:half] += fin_x[:half].astype(F32)
    fy1.wait_recv()
    gw_out[half:] += fin_y[half:].astype(F32)
    fy0.wait_recv()
    gw_out[:half] += fin_y[:half].astype(F32)
    moves.append(pltpu.make_async_copy(gw_out.at[top], gw_hbm.at[top], s_out.at[2]))
    moves[2].start()
    fx1.wait_recv()
    gw_out[half:] += fin_x[half:].astype(F32)
    moves.append(pltpu.make_async_copy(gw_out.at[bottom], gw_hbm.at[bottom], s_out.at[3]))
    moves[3].start()
    for copy in moves:
        copy.wait()
    for copy in pending:
        copy.wait_send()


def move_out(keys, gtok, gw, keys_out, gtok_out, gw_out, sem):
    copies = [
        pltpu.make_async_copy(src, dst, sem.at[n])
        for n, (src, dst) in enumerate(((keys, keys_out), (gtok, gtok_out), (gw, gw_out)))
    ]
    for copy in copies:
        copy.start()
    for copy in copies:
        copy.wait()


def cube_body(nz, tokens, seg_ids, key_weight, key_grad):
    toks, depth = tokens.shape
    rows, width = key_weight.shape[0], key_grad.shape[1]
    half = rows // 2
    tile = min(512, depth)
    freq = np.float32(500000.0) ** (-2.0 * np.arange(HEAD // 2, dtype=np.float32) / HEAD)
    freq = jnp.asarray(np.tile(freq.astype(np.float32), 2)[None, :])
    limit = 60 * 1024 * 1024
    hbm = pl.BlockSpec(memory_space=pltpu.HBM)
    dma = pltpu.SemaphoreType.DMA
    far = max(nz - 1, 1)
    shapes = (
        jax.ShapeDtypeStruct((toks, width), BF16),
        jax.ShapeDtypeStruct((toks, depth), BF16),
        jax.ShapeDtypeStruct((rows, depth), F32),
    )
    results = pl.pallas_call(
        functools.partial(cube_kernel, nz, tile),
        out_shape=shapes,
        in_specs=[hbm] * 5,
        out_specs=(hbm,) * 3,
        scratch_shapes=[
            pltpu.VMEM((toks, width), BF16),
            pltpu.VMEM((toks, depth), BF16),
            pltpu.VMEM((rows, depth), F32),
            pltpu.VMEM((toks, depth), BF16),
            pltpu.VMEM(seg_ids.shape, jnp.int32),
            pltpu.VMEM(key_grad.shape, BF16),
            pltpu.VMEM(freq.shape, F32),
            pltpu.VMEM((width, depth), BF16),
            pltpu.VMEM((toks, depth), BF16),
            pltpu.VMEM((width, toks), BF16),
            pltpu.VMEM((width, toks), BF16),
            pltpu.VMEM((toks, width), BF16),
            pltpu.VMEM((toks, HEAD), F32),
            pltpu.VMEM((toks, HEAD), F32),
            pltpu.VMEM((3, rows, depth), BF16),
            pltpu.VMEM((2, half, depth), F32),
            pltpu.VMEM((half, depth), BF16),
            pltpu.VMEM((half, depth), BF16),
            pltpu.VMEM((rows, depth), BF16),
            pltpu.VMEM((rows, depth), BF16),
            pltpu.VMEM((toks, width), F32),
            pltpu.VMEM((far, toks // nz, width), F32),
            dma((6,)), dma((6,)),
            dma((9,)), dma((9,)),
            dma((6,)), dma((6,)),
            dma((far,)), dma((far,)),
            dma((far,)), dma((far,)),
            dma((5,)), dma((4,)),
        ],
        compiler_params=pltpu.CompilerParams(
            collective_id=0, has_side_effects=True, vmem_limit_bytes=limit
        ),
        cost_estimate=pl.CostEstimate(
            flops=6 * toks * width * depth,
            bytes_accessed=4 * toks * depth + 6 * rows * depth,
            transcendentals=2 * toks * HEAD,
        ),
    )(tokens, seg_ids, key_weight, key_grad, freq)
    return pl.pallas_call(
        move_out,
        out_shape=shapes,
        in_specs=[hbm] * 3,
        out_specs=(hbm,) * 3,
        scratch_shapes=[dma((3,))],
        compiler_params=pltpu.CompilerParams(vmem_limit_bytes=limit),
        cost_estimate=pl.CostEstimate(
            flops=0, bytes_accessed=2 * toks * depth + 4 * rows * depth, transcendentals=0
        ),
    )(*results)


def solution(mesh):
    nz = mesh.shape["tensor"]
    body = plain_body
    if mesh.shape["fsdp"] == 8 and nz <= 8:
        body = functools.partial(cube_body, nz)
    placed = (P("fsdp", "tensor"), P("fsdp", None), P("fsdp", "tensor"), P("fsdp", None))
    return jax.shard_map(
        body,
        mesh=mesh,
        in_specs=placed,
        out_specs=(P("fsdp", None), P("fsdp", "tensor"), P("fsdp", "tensor")),
        check_vma=False,
    )
```

```python
import functools

import jax
import jax.numpy as jnp
import numpy as np
from jax import lax
from jax.experimental import pallas as pl
from jax.experimental.pallas import tpu as pltpu
from jax.sharding import PartitionSpec as P

HEAD = 128
MESH = pl.DeviceIdType.MESH
F32 = jnp.float32
BF16 = jnp.bfloat16


def doc_positions(segments):
    width = segments.shape[0]
    index = jnp.arange(width, dtype=jnp.int32)
    change = jnp.concatenate([jnp.ones((1,), bool), segments[1:] != segments[:-1]])
    first = lax.cummax(jnp.where(change, index, 0))
    return index - first


def angles(positions, half):
    freq = 500000.0 ** (-2.0 * jnp.arange(half, dtype=jnp.float32) / (2 * half))
    turn = positions.astype(jnp.float32)[:, None] * freq[None, :]
    return (jnp.cos(turn)[:, None, :], jnp.sin(turn)[:, None, :])


def rotate(field, cosine, sine, sign):
    rows = field.shape[0]
    shaped = field.reshape(rows, -1, HEAD)
    first, second = (shaped[..., : HEAD // 2], shaped[..., HEAD // 2 :])
    out = jnp.concatenate(
        [first * cosine - sign * second * sine, second * cosine + sign * first * sine], axis=-1
    )
    return out.reshape(rows, -1)


def plain_body(tokens, seg_ids, key_weight, key_grad):
    cosine, sine = angles(doc_positions(seg_ids[0]), HEAD // 2)
    weights = lax.all_gather(key_weight, "fsdp", axis=0, tiled=True)
    partial_value = lax.dot_general(
        tokens, weights, (((1,), (1,)), ((), ())), preferred_element_type=jnp.float32
    )
    kraw = lax.psum(partial_value, "tensor")
    keys = rotate(kraw, cosine, sine, 1.0).astype(jnp.bfloat16)
    kback = rotate(key_grad.astype(jnp.float32), cosine, sine, -1.0).astype(jnp.bfloat16)
    grad_tokens = jnp.dot(kback, weights, preferred_element_type=jnp.float32)
    grad_key_weight = lax.psum_scatter(
        lax.dot_general(
            kback, tokens, (((0,), (0,)), ((), ())), preferred_element_type=jnp.float32
        ),
        "fsdp",
        scatter_dimension=0,
        tiled=True,
    )
    return (keys, grad_tokens.astype(jnp.bfloat16), grad_key_weight)


def turned(block, cosine, signed_sine):
    return block * cosine + pltpu.roll(block, HEAD // 2, 1) * signed_sine


def cube_kernel(
    nz, tile,
    tok_hbm, seg_hbm, w, kg_hbm, freq_hbm,
    keys_hbm, gtok_hbm, gw_hbm,
    keyb, gtok_out, gw_out, tok, seg, kg, freq, wall, tok_sib, kbt, kbt_sib, kb, cos_s, sin_s, snd, comb, from_x, from_y, fin_x, fin_y,
    kraw, zin,
    s_ag, r_ag, s_sib, r_sib, s_rs, r_rs, s_z, r_z, s_k, r_k, s_in, s_out,
):
    f, t = lax.axis_index("fsdp"), lax.axis_index("tensor")
    y, x, c = f // 4, (f // 2) % 2, f % 2
    xn = y * 4 + (1 - x) * 2 + c
    yn = (1 - y) * 4 + x * 2 + c
    dg = (1 - y) * 4 + (1 - x) * 2 + c
    sib = y * 4 + x * 2 + (1 - c)
    rows, depth = w.shape
    half = rows // 2
    toks, heads = tok.shape[0], kg.shape[1] // HEAD
    peers = [lax.rem(t + d, nz) for d in range(1, nz)]

    barrier = pltpu.get_barrier_semaphore()
    for g in (xn, yn, sib):
        pl.semaphore_signal(barrier, inc=1, device_id=(g, t), device_id_type=MESH)
    for p in peers:
        pl.semaphore_signal(barrier, inc=1, device_id=(f, p), device_id_type=MESH)
    own_rows = pl.ds(pl.multiple_of(f * rows, rows), rows)
    loads = [
        pltpu.make_async_copy(src, dst, s_in.at[n])
        for n, (src, dst) in enumerate(
            ((seg_hbm, seg), (freq_hbm, freq), (kg_hbm, kg), (tok_hbm, tok), (w, wall.at[own_rows]))
        )
    ]
    for load in loads:
        load.start()
    pl.semaphore_wait(barrier, 3 + len(peers))

    pending = []

    def send(src, dst, ssem, rsem, g, p):
        copy = pltpu.make_async_remote_copy(
            src_ref=src, dst_ref=dst, send_sem=ssem, recv_sem=rsem,
            device_id=(g, p), device_id_type=MESH,
        )
        copy.start()
        pending.append(copy)
        return copy

    def shard_half(g, h):
        return wall.at[pl.ds(pl.multiple_of(g * rows + h * half, half), half)]

    def w_half(h):
        return w.at[pl.ds(h * half, half)]

    ax, ay = [None, None], [None, None]
    ax[0] = send(w_half(0), shard_half(f, 0), s_ag.at[0], r_ag.at[0], xn, t)
    ay[1] = send(w_half(1), shard_half(f, 1), s_ag.at[3], r_ag.at[3], yn, t)
    tok_copy = send(tok_hbm, tok_sib, s_sib.at[0], r_sib.at[0], sib, t)
    ax[1] = send(w_half(1), shard_half(f, 1), s_ag.at[1], r_ag.at[1], xn, t)
    ay[0] = send(w_half(0), shard_half(f, 0), s_ag.at[2], r_ag.at[2], yn, t)
    own_copy = send(w, wall.at[own_rows], s_sib.at[2], r_sib.at[2], sib, t)

    for load in loads[:3]:
        load.wait()
    ids = jnp.broadcast_to(seg[...].astype(F32), (toks, toks))
    row = lax.broadcasted_iota(jnp.int32, (toks, toks), 0)
    col = lax.broadcasted_iota(jnp.int32, (toks, toks), 1)
    same = jnp.where((ids == ids.T) & (col < row), 1.0, 0.0)
    position = jnp.sum(same, axis=1, keepdims=True)
    turn = position * freq[...]
    lane = lax.broadcasted_iota(jnp.int32, (toks, HEAD), 1)
    cosine = jnp.cos(turn)
    sine = jnp.sin(turn)
    sine = jnp.where(lane < HEAD // 2, -sine, sine)
    cos_s[...] = cosine
    sin_s[...] = sine
    for h in range(heads):
        lanes = pl.ds(h * HEAD, HEAD)
        back = turned(kg[:, lanes].astype(F32), cosine, -sine).astype(BF16)
        kb[:, lanes] = back
        kbt[lanes, :] = back.astype(F32).T.astype(BF16)
    kb_copy = send(kbt, kbt_sib, s_sib.at[1], r_sib.at[1], sib, t)

    for load in loads[3:]:
        load.wait()
    tok_copy.wait_recv()
    kb_copy.wait_recv()
    picked = []
    for g in (dg, xn, yn, f):
        at = pl.ds(pl.multiple_of(g * rows, rows), rows)
        picked.append(jnp.concatenate([kbt[at, :], kbt_sib[at, :]], axis=1))
    left = jnp.concatenate(picked, axis=0)

    @pl.loop(0, depth // tile)
    def _(i):
        lanes = pl.ds(pl.multiple_of(i * tile, tile), tile)
        right = jnp.concatenate([tok[:, lanes], tok_sib[:, lanes]], axis=0)
        part = jnp.dot(left, right, preferred_element_type=F32)
        snd[0, :, lanes] = part[:rows].astype(BF16)
        snd[1, :half, lanes] = part[rows : rows + half].astype(BF16)
        comb[0, :, lanes] = part[rows + half : 2 * rows]
        comb[1, :, lanes] = part[2 * rows : 2 * rows + half]
        snd[2, half:, lanes] = part[2 * rows + half : 3 * rows].astype(BF16)
        gw_out[:, lanes] = part[3 * rows :]

    sib_waits = [own_copy]

    def to_sib(g, h, n):
        sib_waits.append(
            send(shard_half(g, h), shard_half(g, h), s_sib.at[n], r_sib.at[n], sib, t)
        )

    ax[0].wait_recv()
    ad0 = send(shard_half(xn, 0), shard_half(xn, 0), s_ag.at[4], r_ag.at[4], yn, t)
    ay[1].wait_recv()
    ad1 = send(shard_half(yn, 1), shard_half(yn, 1), s_ag.at[5], r_ag.at[5], xn, t)
    to_sib(xn, 0, 3)
    to_sib(yn, 1, 4)

    ax[1].wait_recv()
    to_sib(xn, 1, 5)
    ay[0].wait_recv()
    to_sib(yn, 0, 6)
    top, bottom = pl.ds(0, half), pl.ds(half, half)
    rdx = send(snd.at[0, top], from_x, s_rs.at[0], r_rs.at[0], xn, t)
    rdy = send(snd.at[0, bottom], from_y, s_rs.at[1], r_rs.at[1], yn, t)
    fx0 = send(snd.at[1, top], fin_x.at[top], s_rs.at[2], r_rs.at[2], xn, t)
    fy1 = send(snd.at[2, bottom], fin_y.at[bottom], s_rs.at[3], r_rs.at[3], yn, t)

    ad0.wait_recv()
    to_sib(dg, 0, 7)
    ad1.wait_recv()
    to_sib(dg, 1, 8)
    for copy in sib_waits:
        copy.wait_recv()

    kraw[...] = jnp.zeros_like(kraw)

    @pl.loop(0, depth // tile)
    def _(i):
        lanes = pl.ds(pl.multiple_of(i * tile, tile), tile)
        kraw[...] += lax.dot_general(
            tok[:, lanes], wall[:, lanes], (((1,), (1,)), ((), ())), preferred_element_type=F32
        )

    share = toks // nz

    def rows_of(p):
        return pl.ds(pl.multiple_of(p * share, share), share)

    z_copies = [
        send(kraw.at[rows_of(p)], zin.at[d], s_z.at[d], r_z.at[d], f, p)
        for d, p in enumerate(peers)
    ]

    rdx.wait_recv()
    snd[2, :half] = (comb[1] + from_x[...].astype(F32)).astype(BF16)
    fy0 = send(snd.at[2, top], fin_y.at[top], s_rs.at[4], r_rs.at[4], yn, t)
    rdy.wait_recv()
    snd[1, half:] = (comb[0] + from_y[...].astype(F32)).astype(BF16)
    fx1 = send(snd.at[1, bottom], fin_x.at[bottom], s_rs.at[5], r_rs.at[5], xn, t)

    mine = rows_of(t)
    total = kraw[mine, :]
    for d, copy in enumerate(z_copies):
        copy.wait_recv()
        total = total + zin[d]
    cosine, sine = cos_s[mine, :], sin_s[mine, :]
    for h in range(heads):
        keyb[mine, h * HEAD : (h + 1) * HEAD] = turned(
            total[:, h * HEAD : (h + 1) * HEAD], cosine, sine
        ).astype(BF16)
    k_copies = [
        send(keyb.at[mine], keyb.at[mine], s_k.at[d], r_k.at[d], f, p)
        for d, p in enumerate(peers)
    ]

    @pl.loop(0, depth // tile)
    def _(i):
        lanes = pl.ds(pl.multiple_of(i * tile, tile), tile)
        gtok_out[:, lanes] = jnp.dot(
            kb[...], wall[:, lanes], preferred_element_type=F32
        ).astype(BF16)

    moves = [pltpu.make_async_copy(gtok_out, gtok_hbm, s_out.at[0])]
    moves[0].start()
    for copy in k_copies:
        copy.wait_recv()
    moves.append(pltpu.make_async_copy(keyb, keys_hbm, s_out.at[1]))
    moves[1].start()

    fx0.wait_recv()
    gw_out[:half] += fin_x[:half].astype(F32)
    fy1.wait_recv()
    gw_out[half:] += fin_y[half:].astype(F32)
    fy0.wait_recv()
    gw_out[:half] += fin_y[:half].astype(F32)
    moves.append(pltpu.make_async_copy(gw_out.at[top], gw_hbm.at[top], s_out.at[2]))
    moves[2].start()
    fx1.wait_recv()
    gw_out[half:] += fin_x[half:].astype(F32)
    moves.append(pltpu.make_async_copy(gw_out.at[bottom], gw_hbm.at[bottom], s_out.at[3]))
    moves[3].start()
    for copy in moves:
        copy.wait()
    for copy in pending:
        copy.wait_send()


def move_out(keys, gtok, gw, keys_out, gtok_out, gw_out, keys_v, gtok_v, gw_v, s_in, s_out):
    whole = ((gw, gw_v, gw_out), (gtok, gtok_v, gtok_out), (keys, keys_v, keys_out))
    ins = [pltpu.make_async_copy(a, v, s_in.at[n]) for n, (a, v, _) in enumerate(whole)]
    outs = [pltpu.make_async_copy(v, b, s_out.at[n]) for n, (_, v, b) in enumerate(whole)]
    for copy in ins:
        copy.start()
    for arrived, leaving in zip(ins, outs):
        arrived.wait()
        leaving.start()
    for copy in outs:
        copy.wait()


def cube_body(nz, tokens, seg_ids, key_weight, key_grad):
    toks, depth = tokens.shape
    rows, width = key_weight.shape[0], key_grad.shape[1]
    half = rows // 2
    tile = min(512, depth)
    freq = np.float32(500000.0) ** (-2.0 * np.arange(HEAD // 2, dtype=np.float32) / HEAD)
    freq = jnp.asarray(np.tile(freq.astype(np.float32), 2)[None, :])
    limit = 60 * 1024 * 1024
    hbm = pl.BlockSpec(memory_space=pltpu.HBM)
    dma = pltpu.SemaphoreType.DMA
    far = max(nz - 1, 1)
    shapes = (
        jax.ShapeDtypeStruct((toks, width), BF16),
        jax.ShapeDtypeStruct((toks, depth), BF16),
        jax.ShapeDtypeStruct((rows, depth), F32),
    )
    results = pl.pallas_call(
        functools.partial(cube_kernel, nz, tile),
        out_shape=shapes,
        in_specs=[hbm] * 5,
        out_specs=(hbm,) * 3,
        scratch_shapes=[
            pltpu.VMEM((toks, width), BF16),
            pltpu.VMEM((toks, depth), BF16),
            pltpu.VMEM((rows, depth), F32),
            pltpu.VMEM((toks, depth), BF16),
            pltpu.VMEM(seg_ids.shape, jnp.int32),
            pltpu.VMEM(key_grad.shape, BF16),
            pltpu.VMEM(freq.shape, F32),
            pltpu.VMEM((width, depth), BF16),
            pltpu.VMEM((toks, depth), BF16),
            pltpu.VMEM((width, toks), BF16),
            pltpu.VMEM((width, toks), BF16),
            pltpu.VMEM((toks, width), BF16),
            pltpu.VMEM((toks, HEAD), F32),
            pltpu.VMEM((toks, HEAD), F32),
            pltpu.VMEM((3, rows, depth), BF16),
            pltpu.VMEM((2, half, depth), F32),
            pltpu.VMEM((half, depth), BF16),
            pltpu.VMEM((half, depth), BF16),
            pltpu.VMEM((rows, depth), BF16),
            pltpu.VMEM((rows, depth), BF16),
            pltpu.VMEM((toks, width), F32),
            pltpu.VMEM((far, toks // nz, width), F32),
            dma((6,)), dma((6,)),
            dma((9,)), dma((9,)),
            dma((6,)), dma((6,)),
            dma((far,)), dma((far,)),
            dma((far,)), dma((far,)),
            dma((5,)), dma((4,)),
        ],
        compiler_params=pltpu.CompilerParams(
            collective_id=0, has_side_effects=True, vmem_limit_bytes=limit
        ),
        cost_estimate=pl.CostEstimate(
            flops=6 * toks * width * depth,
            bytes_accessed=4 * toks * depth + 6 * rows * depth,
            transcendentals=2 * toks * HEAD,
        ),
    )(tokens, seg_ids, key_weight, key_grad, freq)
    return pl.pallas_call(
        move_out,
        out_shape=shapes,
        in_specs=[hbm] * 3,
        out_specs=(hbm,) * 3,
        scratch_shapes=[pltpu.VMEM(a.shape, a.dtype) for a in shapes] + [dma((3,)), dma((3,))],
        compiler_params=pltpu.CompilerParams(vmem_limit_bytes=limit),
        cost_estimate=pl.CostEstimate(
            flops=0, bytes_accessed=2 * toks * depth + 4 * rows * depth, transcendentals=0
        ),
    )(*results)


def solution(mesh):
    nz = mesh.shape["tensor"]
    body = plain_body
    if mesh.shape["fsdp"] == 8 and nz <= 8:
        body = functools.partial(cube_body, nz)
    placed = (P("fsdp", "tensor"), P("fsdp", None), P("fsdp", "tensor"), P("fsdp", None))
    return jax.shard_map(
        body,
        mesh=mesh,
        in_specs=placed,
        out_specs=(P("fsdp", None), P("fsdp", "tensor"), P("fsdp", "tensor")),
        check_vma=False,
    )
```
